32 devices in a mesh: pool: 4 (over z), grid: 4 (over y, x), blk: 2 (over core).
Axes of the slice: x: 2, y: 2, z: 4, core: 2. Of those that a mesh axis runs over, the one named last changes fastest.
Arguments:
- pot_slab: float32 [512, 256], P(('pool', 'grid', 'blk')), may hold values from -6 to 6
- orbitals: bfloat16 [512, 256, 256], P(('pool', 'grid', 'blk')), may hold values from -0.3984375 to 0.3984375
- batch_atoms: int32 [512, 16], P(('pool', 'grid', 'blk')), may hold values from 0 to 23, as said below
- batch_images: int32 [512, 16], P(('pool', 'grid', 'blk')), may hold values from 0 to 1
- phase_index: int32 [8, 2], replicated, may hold values from 0 to 7
Outputs:
- bloch_real: float32 [8, 2304, 256], P('pool', ('grid', 'blk'))
- bloch_imag: float32 [8, 2304, 256], P('pool', ('grid', 'blk'))
The draws below stay inside these ranges and needn't reach their ends.
Inputs may be any that keep to these rules, and one draw needn't show every extreme that they name: `batch_atoms`: each row names 16 different atoms of the batch's region.
All inputs are finite; a program needn't handle non-finite values.
Results may differ from the reference program's by a relative error of at most 0.0029.
Values sent between devices are 32-bit elements; how exact they have to be, the bound alone decides.
A program may use at most 192 MiB of HBM per device.

```python
import math
import jax
import jax.numpy as jnp
from jax import lax

PTS = 256
NAO = 16
BATOMS = 16
ATOMS_G = 24
NR = 2
KGRID = 8
BDEV = 16
BATCHES = 512
NK = 8
TILES_G = 576
N_POOL = 4
N_GRID = 4
N_BLK = 2


def draw_batch_atoms(key, part):
    key = jax.random.fold_in(key, 11)
    scores = jax.random.randint(key, (BATCHES, ATOMS_G), 0, 1 << 20)
    scores = scores * ATOMS_G + jnp.arange(ATOMS_G, dtype=jnp.int32)[None, :]
    ordering = jnp.argsort(scores, axis=1, stable=True)
    return ordering[:, :BATOMS].astype(jnp.int32)


def place_ends(entries, rng, smallest, top_value):
    longest = entries.shape.index(max(entries.shape))
    spots = []
    for shift in (0, 1):
        where = [jax.random.randint(jax.random.fold_in(rng, axis), (), 0, length) for axis, length in enumerate(entries.shape)]
        where[longest] = (where[longest] + shift) % entries.shape[longest]
        spots.append(tuple(where))
    return entries.at[spots[0]].set(smallest).at[spots[1]].set(top_value)


def block_levels(rng, extent, cuts, low, top_value):
    level = 1.0
    for dim, blocks in cuts:
        steps = jax.random.uniform(jax.random.fold_in(jax.random.fold_in(rng, 6), dim), (blocks,), jnp.float32, low / len(cuts), top_value / len(cuts))
        level = level * jnp.repeat(jnp.exp(steps), extent[dim] // blocks).reshape((-1,) + (1,) * (len(extent) - 1 - dim))
    return level


def gaussian(key, shape, scale, reach, shards=(), kind=jnp.bfloat16):
    factor_of = block_levels(key, shape, shards, -0.22, 0.18) if shards else 1.0
    values = jax.random.normal(key, shape, jnp.float32) * scale * factor_of
    return jnp.minimum(jnp.maximum(values, -reach), reach).astype(kind)


def setup_inputs(seed: int = 0) -> dict:
    streams_of = jax.random.split(jax.random.key(seed), 6)
    pot_slab = gaussian(streams_of[0], (BATCHES, PTS), 1.0, 6.0, ((0, 32),), jnp.float32)
    orbitals = gaussian(streams_of[1], (BATCHES, BATOMS * NAO, PTS), 0.065, 0.3984375, ((0, 32),))
    batch_atoms = draw_batch_atoms(jax.random.fold_in(streams_of[5], 71), 0)
    batch_images = place_ends(jax.random.randint(streams_of[3], (BATCHES, BATOMS), 0, NR), jax.random.fold_in(streams_of[3], 1), 0, NR - 1).astype(jnp.int32)
    phase_index = place_ends(jax.random.randint(streams_of[4], (NK, NR), 0, KGRID), jax.random.fold_in(streams_of[4], 1), 0, KGRID - 1).astype(jnp.int32)
    return dict(pot_slab=pot_slab, orbitals=orbitals, batch_atoms=batch_atoms, batch_images=batch_images, phase_index=phase_index)


def reference(pot_slab, orbitals, batch_atoms, batch_images, phase_index):
    per_owner = BDEV // N_GRID
    potential = pot_slab.reshape(N_POOL, N_GRID, N_BLK, N_GRID, per_owner, PTS)
    potential = potential.transpose(0, 3, 2, 1, 4, 5).reshape(BATCHES, PTS)
    block_width = NAO * NAO

    def one_device(summed, device_index):
        first_row = device_index * BDEV
        orbital_block = lax.dynamic_slice_in_dim(orbitals, first_row, BDEV, 0)
        potential_block = lax.dynamic_slice_in_dim(potential, first_row, BDEV, 0)
        atom_block = lax.dynamic_slice_in_dim(batch_atoms, first_row, BDEV, 0)
        image_block = lax.dynamic_slice_in_dim(batch_images, first_row, BDEV, 0)
        weighted = (orbital_block.astype(jnp.float32) * potential_block[:, None, :]).astype(jnp.bfloat16)
        blocks = jnp.einsum("bip,bjp->bij", weighted.astype(jnp.float32), orbital_block.astype(jnp.float32),
                            precision=lax.Precision.HIGHEST)
        blocks = blocks.reshape(BDEV, BATOMS, NAO, BATOMS, NAO).transpose(0, 1, 3, 2, 4)
        blocks = blocks.reshape(BDEV * BATOMS * BATOMS, block_width)
        region = (device_index // N_BLK) % N_GRID
        tile_index = atom_block[:, :, None] * ATOMS_G + atom_block[:, None, :]
        image_slot = jnp.mod(image_block[:, :, None] - image_block[:, None, :], NR)
        pair_slot = (region * TILES_G + tile_index) * NR + image_slot
        return summed.at[pair_slot.reshape(-1)].add(blocks), None

    device_list = jnp.arange(N_POOL * N_GRID * N_BLK, dtype=jnp.int32)
    summed, _ = lax.scan(one_device, jnp.zeros((N_GRID * TILES_G * NR, block_width), jnp.float32), device_list)
    real_space = summed.reshape(N_GRID * TILES_G, NR, block_width)
    phase_angle = phase_index.astype(jnp.float32) * (2.0 * math.pi / KGRID)
    bloch_real = jnp.einsum("kr,trc->ktc", jnp.cos(phase_angle), real_space, precision=lax.Precision.HIGHEST)
    bloch_imag = jnp.einsum("kr,trc->ktc", jnp.sin(phase_angle), real_space, precision=lax.Precision.HIGHEST)
    return bloch_real, bloch_imag
```

```python
import functools
import math

import jax
import jax.numpy as jnp
from jax import lax
from jax.experimental import pallas as pl
from jax.experimental.pallas import tpu as pltpu
from jax.sharding import PartitionSpec as P

NAO = 16
BATOMS = 16
ATOMS_G = 24
NR = 2
KGRID = 8
CHUNK = 4
LANES = 128
ROWS = ATOMS_G * NAO


def pair_kernel(atoms, images, orb_ref, pot_ref, out_ref, x, w, sx, sw):
    step = pl.program_id(0)
    points = orb_ref.shape[2]
    for ref in (x, w, sx, sw):
        ref[...] = jnp.zeros_like(ref)
    for c in range(CHUNK):
        batch = step * CHUNK + c
        value = pot_ref[pl.ds(batch, 1), :]
        cols = pl.ds(c * points, points)
        for i in range(BATOMS):
            rows = pl.ds(pl.multiple_of(atoms[batch, i] * NAO, NAO), NAO)
            sign = (1 - 2 * images[batch, i]).astype(jnp.float32)
            tile = orb_ref[c, i * NAO : (i + 1) * NAO, :]
            wide = tile.astype(jnp.float32)
            weighted = wide * value
            x[rows, cols] = tile
            w[rows, cols] = weighted.astype(jnp.bfloat16)
            sx[rows, cols] = (wide * sign).astype(jnp.bfloat16)
            sw[rows, cols] = (weighted * sign).astype(jnp.bfloat16)

    @pl.when(step == 0)
    def _():
        out_ref[...] = jnp.zeros_like(out_ref)

    halves = out_ref.shape[0]
    per_half = ROWS // halves
    for which, (left, right) in enumerate(((w, x), (sw, sx))):
        for h in range(halves):
            product = lax.dot_general(
                left[h * per_half : (h + 1) * per_half, :],
                right[...],
                (((1,), (1,)), ((), ())),
                preferred_element_type=jnp.float32,
            )
            for n in range(ROWS // LANES):
                out_ref[h, which, n] += product[:, n * LANES : (n + 1) * LANES]


def pair_matrices(orbitals, potential, batch_atoms, batch_images, halves):
    batches, rows, points = orbitals.shape
    wide = CHUNK * points
    return pl.pallas_call(
        pair_kernel,
        out_shape=jax.ShapeDtypeStruct((halves, 2, ROWS // LANES, ROWS // halves, LANES), jnp.float32),
        grid_spec=pltpu.PrefetchScalarGridSpec(
            num_scalar_prefetch=2,
            grid=(batches // CHUNK,),
            in_specs=[
                pl.BlockSpec((CHUNK, rows, points), lambda s, *_: (s, 0, 0)),
                pl.BlockSpec((batches, points), lambda s, *_: (0, 0)),
            ],
            out_specs=pl.BlockSpec((halves, 2, ROWS // LANES, ROWS // halves, LANES), lambda s, *_: (0,) * 5),
            scratch_shapes=[pltpu.VMEM((ROWS, wide), jnp.bfloat16)] * 4,
        ),
        compiler_params=pltpu.CompilerParams(vmem_limit_bytes=40 << 20),
    )(batch_atoms, batch_images, orbitals, potential)


def tile_kernel(coef, h_ref, re_ref, im_ref, tiles):
    own = h_ref.shape[2] // NAO
    slots = LANES // NAO
    lane_slot = lax.broadcasted_iota(jnp.int32, (own, LANES), 1) // NAO
    for which in range(2):
        for b in range(ATOMS_G):
            for half in range(NAO // slots):
                total = None
                for s in range(slots):
                    piece = h_ref[which, b // slots, pl.ds(half * slots + s, own, stride=NAO), :]
                    shift = (s - b % slots) * NAO % LANES
                    if shift:
                        piece = pltpu.roll(piece, shift, 1)
                    total = piece if total is None else jnp.where(lane_slot == s, piece, total)
                tiles[which, half, pl.ds(b, own, stride=ATOMS_G), :] = total
    for half in range(NAO // slots):
        lanes = pl.ds(half * LANES, LANES)
        plus, minus = tiles[0, half], tiles[1, half]
        for k in range(re_ref.shape[0]):
            re_ref[k, :, lanes] = coef[k, 0] * plus + coef[k, 1] * minus
            im_ref[k, :, lanes] = coef[k, 2] * plus + coef[k, 3] * minus


def bloch_tiles(coef, owned):
    tile_rows = owned.shape[2] // NAO * ATOMS_G
    shape = jax.ShapeDtypeStruct((coef.shape[0], tile_rows, NAO * NAO), jnp.float32)
    vmem = pl.BlockSpec(memory_space=pltpu.VMEM)
    return pl.pallas_call(
        tile_kernel,
        out_shape=(shape, shape),
        in_specs=[pl.BlockSpec(memory_space=pltpu.SMEM), vmem],
        out_specs=(vmem, vmem),
        scratch_shapes=[pltpu.VMEM((2, NAO * NAO // LANES, tile_rows, LANES), jnp.float32)],
        compiler_params=pltpu.CompilerParams(vmem_limit_bytes=40 << 20),
    )(coef, owned)


def phase_coefficients(phase_index, per_pool):
    mine = lax.dynamic_slice_in_dim(phase_index, lax.axis_index("pool") * per_pool, per_pool, 0)
    angle = mine.astype(jnp.float32) * (2.0 * math.pi / KGRID)
    cos, sin = jnp.cos(angle) * 0.5, jnp.sin(angle) * 0.5
    return jnp.stack(
        [cos[:, 0] + cos[:, 1], cos[:, 0] - cos[:, 1], sin[:, 0] + sin[:, 1], sin[:, 0] - sin[:, 1]], axis=1
    )


def per_device(pot_slab, orbitals, batch_atoms, batch_images, phase_index):
    grid_size = lax.axis_size("grid")
    pool_size = lax.axis_size("pool")
    blk_size = lax.axis_size("blk")
    row_count, points = pot_slab.shape
    pieces = pot_slab.reshape(grid_size, row_count // grid_size, points)
    arrived = lax.all_to_all(pieces, "grid", split_axis=0, concat_axis=0, tiled=True)
    potential = arrived.reshape(row_count, points)
    pairs = pair_matrices(orbitals, potential, batch_atoms, batch_images, blk_size)
    coef = phase_coefficients(phase_index, phase_index.shape[0] // pool_size)
    flat = pairs.reshape(-1, LANES)
    summed = lax.psum_scatter(flat, ("blk", "pool"), scatter_dimension=0, tiled=True)
    owned = lax.all_gather(summed, "pool", axis=0, tiled=True)
    return bloch_tiles(coef, owned.reshape(pairs.shape[1:]))


def solution(mesh):
    in_specs = (
        P(("pool", "grid", "blk"), None),
        P(("pool", "grid", "blk"), None, None),
        P(("pool", "grid", "blk"), None),
        P(("pool", "grid", "blk"), None),
        P(),
    )
    out_specs = (P("pool", ("grid", "blk"), None), P("pool", ("grid", "blk"), None))
    return jax.shard_map(
        per_device, mesh=mesh, in_specs=in_specs, out_specs=out_specs, check_vma=False
    )
```

```python
import functools
import math

import jax
import jax.numpy as jnp
from jax import lax
from jax.experimental import pallas as pl
from jax.experimental.pallas import tpu as pltpu
from jax.sharding import PartitionSpec as P

NAO = 16
BATOMS = 16
ATOMS_G = 24
NR = 2
KGRID = 8
CHUNK = 4
LANES = 128
ROWS = ATOMS_G * NAO
PARTS = ROWS // LANES
BLOCKS = PARTS * (PARTS + 1) // 2
MESH = pl.DeviceIdType.MESH


def swap_kernel(size, pot_ref, out_ref, send, land, send_sem, recv_sem):
    me = lax.axis_index("grid")
    barrier = pltpu.get_barrier_semaphore()
    for d in range(1, size):
        pl.semaphore_signal(barrier, inc=1, device_id={"grid": lax.rem(me + d, size)}, device_id_type=MESH)
    rows = pot_ref.shape[0] // size
    for j in range(size):
        send[j] = pot_ref[j * rows : (j + 1) * rows, :]
    pl.semaphore_wait(barrier, size - 1)
    copies = []
    for d in range(1, size):
        to = lax.rem(me + d, size)
        copies.append(
            pltpu.make_async_remote_copy(
                src_ref=send.at[to],
                dst_ref=land.at[d],
                send_sem=send_sem.at[d],
                recv_sem=recv_sem.at[d],
                device_id={"grid": to},
                device_id_type=MESH,
            )
        )
        copies[-1].start()
    land[0] = send[me]
    for copy in copies:
        copy.wait()
    for j in range(size):
        out_ref[j * rows : (j + 1) * rows, :] = land[lax.rem(me - j + size, size)]


def batch_potential(pot_slab, size):
    rows, points = pot_slab.shape
    vmem = pl.BlockSpec(memory_space=pltpu.VMEM)
    return pl.pallas_call(
        functools.partial(swap_kernel, size),
        out_shape=jax.ShapeDtypeStruct(pot_slab.shape, pot_slab.dtype),
        in_specs=[vmem],
        out_specs=vmem,
        scratch_shapes=[pltpu.VMEM((size, rows // size, points), jnp.float32)] * 2
        + [pltpu.SemaphoreType.DMA((size,))] * 2,
        compiler_params=pltpu.CompilerParams(collective_id=0, has_side_effects=True),
    )(pot_slab)


def pair_kernel(atoms, images, orb_ref, pot_ref, out_ref, x, w, sx, sw):
    step = pl.program_id(0)
    points = orb_ref.shape[2]
    for ref in (x, w, sx, sw):
        ref[...] = jnp.zeros_like(ref)
    for c in range(CHUNK):
        batch = step * CHUNK + c
        value = pot_ref[pl.ds(batch, 1), :]
        cols = pl.ds(c * points, points)
        for i in range(BATOMS):
            rows = pl.ds(pl.multiple_of(atoms[batch, i] * NAO, NAO), NAO)
            sign = (1 - 2 * images[batch, i]).astype(jnp.float32)
            tile = orb_ref[c, i * NAO : (i + 1) * NAO, :]
            wide = tile.astype(jnp.float32)
            weighted = wide * value
            x[rows, cols] = tile
            w[rows, cols] = weighted.astype(jnp.bfloat16)
            sx[rows, cols] = (wide * sign).astype(jnp.bfloat16)
            sw[rows, cols] = (weighted * sign).astype(jnp.bfloat16)

    @pl.when(step == 0)
    def _():
        out_ref[...] = jnp.zeros_like(out_ref)

    for which, (left, right) in enumerate(((w, x), (sw, sx))):
        index = 0
        for r in range(PARTS):
            product = lax.dot_general(
                left[r * LANES : (r + 1) * LANES, :],
                right[r * LANES :, :],
                (((1,), (1,)), ((), ())),
                preferred_element_type=jnp.float32,
            )
            for n in range(PARTS - r):
                out_ref[which, index] += product[:, n * LANES : (n + 1) * LANES]
                index += 1


def pair_matrices(orbitals, potential, batch_atoms, batch_images):
    batches, rows, points = orbitals.shape
    wide = CHUNK * points
    return pl.pallas_call(
        pair_kernel,
        out_shape=jax.ShapeDtypeStruct((2, BLOCKS, LANES, LANES), jnp.float32),
        grid_spec=pltpu.PrefetchScalarGridSpec(
            num_scalar_prefetch=2,
            grid=(batches // CHUNK,),
            in_specs=[
                pl.BlockSpec((CHUNK, rows, points), lambda s, *_: (s, 0, 0)),
                pl.BlockSpec((batches, points), lambda s, *_: (0, 0)),
            ],
            out_specs=pl.BlockSpec((2, BLOCKS, LANES, LANES), lambda s, *_: (0,) * 4),
            scratch_shapes=[pltpu.VMEM((ROWS, wide), jnp.bfloat16)] * 4,
        ),
        compiler_params=pltpu.CompilerParams(vmem_limit_bytes=40 << 20),
    )(batch_atoms, batch_images, orbitals, potential)


def sum_kernel(
    size, mine_ref, out_ref, from_core, own, from_left, from_right, to_right, to_left, other, sends, recvs
):
    me, core = lax.axis_index("pool"), lax.axis_index("blk")
    right, left = lax.rem(me + 1, size), lax.rem(me + size - 1, size)
    has_left, has_right = me > 0, me < size - 1
    barrier = pltpu.get_barrier_semaphore()
    for there in ({"blk": 1 - core}, {"pool": left}, {"pool": right}):
        pl.semaphore_signal(barrier, inc=1, device_id=there, device_id_type=MESH)

    def copy(way, src, dst, c, there):
        return pltpu.make_async_remote_copy(
            src_ref=src,
            dst_ref=dst.at[c],
            send_sem=sends.at[way, c],
            recv_sem=recvs.at[way, c],
            device_id=there,
            device_id_type=MESH,
        )

    def core_copy(c):
        return copy(0, mine_ref.at[1 - core, c], from_core, c, {"blk": 1 - core})

    def right_copy(c):
        return copy(1, to_right.at[c], from_left, c, {"pool": right})

    def left_copy(c):
        return copy(2, to_left.at[c], from_right, c, {"pool": left})

    def swap_copy(c):
        return copy(3, out_ref.at[core, c], other, c, {"blk": 1 - core})

    pl.semaphore_wait(barrier, 3)
    for c in range(BLOCKS):
        core_copy(c).start()

    @pl.when(me == 0)
    def _():
        from_left[...] = jnp.zeros_like(from_left)

    @pl.when(me == size - 1)
    def _():
        from_right[...] = jnp.zeros_like(from_right)

    behind = size - 1 - me
    near, far = jnp.minimum(me, behind), jnp.maximum(me, behind)

    def step(t, carry):
        c0, c1, c2, c3 = t - near, t - me, t - behind, t - far

        @pl.when((c0 >= 0) & (c0 < BLOCKS))
        def _():
            core_copy(c0).wait_recv()
            own[c0] = mine_ref[core, c0] + from_core[c0]

        @pl.when((c1 >= 0) & (c1 < BLOCKS))
        def _():
            @pl.when(has_left)
            def _():
                right_copy(c1).wait_recv()

            @pl.when(has_right)
            def _():
                to_right[c1] = own[c1] + from_left[c1]
                right_copy(c1).start()

        @pl.when((c2 >= 0) & (c2 < BLOCKS))
        def _():
            @pl.when(has_right)
            def _():
                left_copy(c2).wait_recv()

            @pl.when(has_left)
            def _():
                to_left[c2] = own[c2] + from_right[c2]
                left_copy(c2).start()

        @pl.when((c3 >= 0) & (c3 < BLOCKS))
        def _():
            out_ref[core, c3] = from_left[c3] + own[c3] + from_right[c3]
            swap_copy(c3).start()

        return carry

    lax.fori_loop(0, BLOCKS + size - 1, step, 0)
    for c in range(BLOCKS):
        core_copy(c).wait_send()

        @pl.when(has_right)
        def _():
            right_copy(c).wait_send()

        @pl.when(has_left)
        def _():
            left_copy(c).wait_send()

        swap_copy(c).wait()
        out_ref[1 - core, c] = other[c]


def summed_blocks(blocks, size):
    vmem = pl.BlockSpec(memory_space=pltpu.VMEM)
    return pl.pallas_call(
        functools.partial(sum_kernel, size),
        out_shape=jax.ShapeDtypeStruct(blocks.shape, blocks.dtype),
        in_specs=[vmem],
        out_specs=vmem,
        scratch_shapes=[pltpu.VMEM((BLOCKS, LANES, LANES), jnp.float32)] * 7
        + [pltpu.SemaphoreType.DMA((4, BLOCKS))] * 2,
        compiler_params=pltpu.CompilerParams(
            collective_id=1, has_side_effects=True, vmem_limit_bytes=40 << 20
        ),
    )(blocks)


def tile_kernel(coef, core, blocks_ref, re_ref, im_ref, full, tiles):
    own = re_ref.shape[1] // ATOMS_G
    slots = LANES // NAO
    first = core[0] * (own * NAO)
    lane_slot = lax.broadcasted_iota(jnp.int32, (own, LANES), 1) // NAO
    for which in range(2):
        index = 0
        for r in range(PARTS):
            for n in range(r, PARTS):
                block = blocks_ref[which, index]
                full[which, n, r * LANES : (r + 1) * LANES, :] = block
                if n > r:
                    full[which, r, n * LANES : (n + 1) * LANES, :] = block.T
                index += 1
    for which in range(2):
        for b in range(ATOMS_G):
            for half in range(NAO // slots):
                total = None
                for s in range(slots):
                    rows = pl.ds(first + half * slots + s, own, stride=NAO)
                    piece = full[which, b // slots, rows, :]
                    shift = (s - b % slots) * NAO % LANES
                    if shift:
                        piece = pltpu.roll(piece, shift, 1)
                    total = piece if total is None else jnp.where(lane_slot == s, piece, total)
                tiles[which, half, pl.ds(b, own, stride=ATOMS_G), :] = total
    for half in range(NAO // slots):
        lanes = pl.ds(half * LANES, LANES)
        plus, minus = tiles[0, half], tiles[1, half]
        for k in range(re_ref.shape[0]):
            re_ref[k, :, lanes] = coef[k, 0] * plus + coef[k, 1] * minus
            im_ref[k, :, lanes] = coef[k, 2] * plus + coef[k, 3] * minus


def bloch_tiles(coef, core, blocks, tile_rows):
    shape = jax.ShapeDtypeStruct((coef.shape[0], tile_rows, NAO * NAO), jnp.float32)
    vmem = pl.BlockSpec(memory_space=pltpu.VMEM)
    smem = pl.BlockSpec(memory_space=pltpu.SMEM)
    return pl.pallas_call(
        tile_kernel,
        out_shape=(shape, shape),
        in_specs=[smem, smem, vmem],
        out_specs=(vmem, vmem),
        scratch_shapes=[
            pltpu.VMEM((2, PARTS, ROWS, LANES), jnp.float32),
            pltpu.VMEM((2, NAO * NAO // LANES, tile_rows, LANES), jnp.float32),
        ],
        compiler_params=pltpu.CompilerParams(vmem_limit_bytes=40 << 20),
    )(coef, core, blocks)


def phase_coefficients(phase_index, per_pool):
    mine = lax.dynamic_slice_in_dim(phase_index, lax.axis_index("pool") * per_pool, per_pool, 0)
    angle = mine.astype(jnp.float32) * (2.0 * math.pi / KGRID)
    cos, sin = jnp.cos(angle) * 0.5, jnp.sin(angle) * 0.5
    return jnp.stack(
        [cos[:, 0] + cos[:, 1], cos[:, 0] - cos[:, 1], sin[:, 0] + sin[:, 1], sin[:, 0] - sin[:, 1]], axis=1
    )


def per_device(pot_slab, orbitals, batch_atoms, batch_images, phase_index):
    grid_size = lax.axis_size("grid")
    pool_size = lax.axis_size("pool")
    blk_size = lax.axis_size("blk")
    potential = batch_potential(pot_slab, grid_size)
    blocks = pair_matrices(orbitals, potential, batch_atoms, batch_images)
    summed = summed_blocks(blocks, pool_size)
    coef = phase_coefficients(phase_index, phase_index.shape[0] // pool_size)
    core = jnp.reshape(lax.axis_index("blk"), (1,)).astype(jnp.int32)
    return bloch_tiles(coef, core, summed, ATOMS_G * ATOMS_G // blk_size)


def solution(mesh):
    in_specs = (
        P(("pool", "grid", "blk"), None),
        P(("pool", "grid", "blk"), None, None),
        P(("pool", "grid", "blk"), None),
        P(("pool", "grid", "blk"), None),
        P(),
    )
    out_specs = (P("pool", ("grid", "blk"), None), P("pool", ("grid", "blk"), None))
    return jax.shard_map(
        per_device, mesh=mesh, in_specs=in_specs, out_specs=out_specs, check_vma=False
    )
```

```python
import functools
import math

import jax
import jax.numpy as jnp
from jax import lax
from jax.experimental import pallas as pl
from jax.experimental.pallas import tpu as pltpu
from jax.sharding import PartitionSpec as P

NAO = 16
BATOMS = 16
ATOMS_G = 24
NR = 2
KGRID = 8
CHUNK = 16
LANES = 128
ROWS = ATOMS_G * NAO
PARTS = ROWS // LANES
BLOCKS = PARTS * (PARTS + 1) // 2
PIECES = 6
SKEW = 2
MESH = pl.DeviceIdType.MESH


def swap_kernel(size, pot_ref, out_ref, send, land, send_sem, recv_sem):
    me = lax.axis_index("grid")
    barrier = pltpu.get_barrier_semaphore()
    for d in range(1, size):
        pl.semaphore_signal(barrier, inc=1, device_id={"grid": lax.rem(me + d, size)}, device_id_type=MESH)
    rows = pot_ref.shape[0] // size
    for j in range(size):
        send[j] = pot_ref[j * rows : (j + 1) * rows, :]
    pl.semaphore_wait(barrier, size - 1)
    copies = []
    for d in range(1, size):
        to = lax.rem(me + d, size)
        copies.append(
            pltpu.make_async_remote_copy(
                src_ref=send.at[to],
                dst_ref=land.at[d],
                send_sem=send_sem.at[d],
                recv_sem=recv_sem.at[d],
                device_id={"grid": to},
                device_id_type=MESH,
            )
        )
        copies[-1].start()
    land[0] = send[me]
    for copy in copies:
        copy.wait()
    for j in range(size):
        out_ref[j * rows : (j + 1) * rows, :] = land[lax.rem(me - j + size, size)]


def batch_potential(pot_slab, size):
    rows, points = pot_slab.shape
    vmem = pl.BlockSpec(memory_space=pltpu.VMEM)
    return pl.pallas_call(
        functools.partial(swap_kernel, size),
        out_shape=jax.ShapeDtypeStruct(pot_slab.shape, pot_slab.dtype),
        in_specs=[vmem],
        out_specs=vmem,
        scratch_shapes=[pltpu.VMEM((size, rows // size, points), jnp.float32)] * 2
        + [pltpu.SemaphoreType.DMA((size,))] * 2,
        compiler_params=pltpu.CompilerParams(collective_id=0, has_side_effects=True),
    )(pot_slab)


def pair_kernel(places, orb_ref, pot_ref, out_ref, x, w, sx, sw):
    step = pl.program_id(0)
    points = orb_ref.shape[2]
    for ref in (x, w, sx, sw):
        ref[...] = jnp.zeros_like(ref)
    for c in range(CHUNK):
        batch = step * CHUNK + c
        value = pot_ref[pl.ds(batch, 1), :]
        cols = pl.ds(c * points, points)
        for i in range(BATOMS):
            place = places[batch, i]
            rows = pl.ds(pl.multiple_of((place >> 1) * NAO, NAO), NAO)
            sign = (1 - 2 * (place & 1)).astype(jnp.float32)
            tile = orb_ref[c, i * NAO : (i + 1) * NAO, :]
            wide = tile.astype(jnp.float32)
            weighted = wide * value
            x[rows, cols] = tile
            w[rows, cols] = weighted.astype(jnp.bfloat16)
            sx[rows, cols] = (wide * sign).astype(jnp.bfloat16)
            sw[rows, cols] = (weighted * sign).astype(jnp.bfloat16)

    @pl.when(step == 0)
    def _():
        out_ref[...] = jnp.zeros_like(out_ref)

    for which, (left, right) in enumerate(((w, x), (sw, sx))):
        whole = lax.dot_general(left[...], right[...], (((1,), (1,)), ((), ())), preferred_element_type=jnp.float32)
        index = 0
        for r in range(PARTS):
            for n in range(r, PARTS):
                out_ref[which, index] += whole[r * LANES : (r + 1) * LANES, n * LANES : (n + 1) * LANES]
                index += 1


def pair_matrices(orbitals, potential, batch_atoms, batch_images):
    batches, rows, points = orbitals.shape
    wide = CHUNK * points
    return pl.pallas_call(
        pair_kernel,
        out_shape=jax.ShapeDtypeStruct((2, BLOCKS, LANES, LANES), jnp.float32),
        grid_spec=pltpu.PrefetchScalarGridSpec(
            num_scalar_prefetch=1,
            grid=(batches // CHUNK,),
            in_specs=[
                pl.BlockSpec((CHUNK, rows, points), lambda s, *_: (s, 0, 0)),
                pl.BlockSpec((batches, points), lambda s, *_: (0, 0)),
            ],
            out_specs=pl.BlockSpec((2, BLOCKS, LANES, LANES), lambda s, *_: (0,) * 4),
            scratch_shapes=[pltpu.VMEM((ROWS, wide), jnp.bfloat16)] * 4,
        ),
        compiler_params=pltpu.CompilerParams(vmem_limit_bytes=40 << 20),
    )(batch_atoms * NR + batch_images, orbitals, potential)


def sum_kernel(
    size, mine_ref, out_ref, from_core, own, from_left, from_right, to_right, to_left, other, sends, recvs
):
    pieces = mine_ref.shape[1]
    me, core = lax.axis_index("pool"), lax.axis_index("blk")
    right, left = lax.rem(me + 1, size), lax.rem(me + size - 1, size)
    has_left, has_right = me > 0, me < size - 1
    barrier = pltpu.get_barrier_semaphore()
    for there in ({"blk": 1 - core}, {"pool": left}, {"pool": right}):
        pl.semaphore_signal(barrier, inc=1, device_id=there, device_id_type=MESH)

    def copy(way, src, dst, c, there):
        return pltpu.make_async_remote_copy(
            src_ref=src,
            dst_ref=dst.at[c],
            send_sem=sends.at[way, c],
            recv_sem=recvs.at[way, c],
            device_id=there,
            device_id_type=MESH,
        )

    def core_copy(c):
        return copy(0, mine_ref.at[1 - core, c], from_core, c, {"blk": 1 - core})

    def right_copy(c):
        return copy(1, to_right.at[c], from_left, c, {"pool": right})

    def left_copy(c):
        return copy(2, to_left.at[c], from_right, c, {"pool": left})

    def swap_copy(c):
        return copy(3, out_ref.at[core, c], other, c, {"blk": 1 - core})

    pl.semaphore_wait(barrier, 3)
    for c in range(pieces):
        core_copy(c).start()

    @pl.when(me == 0)
    def _():
        from_left[...] = jnp.zeros_like(from_left)

    @pl.when(me == size - 1)
    def _():
        from_right[...] = jnp.zeros_like(from_right)

    behind = size - 1 - me
    near, far = jnp.minimum(me, behind), jnp.maximum(me, behind)

    def step(t, carry):
        c0, c1, c2, c3 = t - SKEW * near, t - SKEW * me, t - SKEW * behind, t - SKEW * far

        @pl.when((c0 >= 0) & (c0 < pieces))
        def _():
            core_copy(c0).wait_recv()
            own[c0] = mine_ref[core, c0] + from_core[c0]

        @pl.when((c1 >= 0) & (c1 < pieces))
        def _():
            @pl.when(has_left)
            def _():
                right_copy(c1).wait_recv()

            @pl.when(has_right)
            def _():
                to_right[c1] = own[c1] + from_left[c1]
                right_copy(c1).start()

        @pl.when((c2 >= 0) & (c2 < pieces))
        def _():
            @pl.when(has_right)
            def _():
                left_copy(c2).wait_recv()

            @pl.when(has_left)
            def _():
                to_left[c2] = own[c2] + from_right[c2]
                left_copy(c2).start()

        @pl.when((c3 >= 0) & (c3 < pieces))
        def _():
            out_ref[core, c3] = from_left[c3] + own[c3] + from_right[c3]
            swap_copy(c3).start()

        return carry

    lax.fori_loop(0, pieces + SKEW * (size - 1), step, 0)
    for c in range(pieces):
        core_copy(c).wait_send()

        @pl.when(has_right)
        def _():
            right_copy(c).wait_send()

        @pl.when(has_left)
        def _():
            left_copy(c).wait_send()

        swap_copy(c).wait()
        out_ref[1 - core, c] = other[c]


def summed_blocks(blocks, size):
    vmem = pl.BlockSpec(memory_space=pltpu.VMEM)
    pieces = (PIECES, BLOCKS * LANES // PIECES, LANES)
    summed = pl.pallas_call(
        functools.partial(sum_kernel, size),
        out_shape=jax.ShapeDtypeStruct((2, *pieces), blocks.dtype),
        in_specs=[vmem],
        out_specs=vmem,
        scratch_shapes=[pltpu.VMEM(pieces, jnp.float32)] * 7
        + [pltpu.SemaphoreType.DMA((4, PIECES))] * 2,
        compiler_params=pltpu.CompilerParams(
            collective_id=1, has_side_effects=True, vmem_limit_bytes=40 << 20
        ),
    )(blocks.reshape(2, *pieces))
    return summed.reshape(blocks.shape)


def tile_kernel(coef, core, blocks_ref, re_ref, im_ref, full, tiles):
    own = re_ref.shape[1] // ATOMS_G
    slots = LANES // NAO
    first = core[0] * (own * NAO)
    lane_slot = lax.broadcasted_iota(jnp.int32, (own, LANES), 1) // NAO
    for which in range(2):
        index = 0
        for r in range(PARTS):
            for n in range(r, PARTS):
                block = blocks_ref[which, index]
                full[which, n, r * LANES : (r + 1) * LANES, :] = block
                if n > r:
                    full[which, r, n * LANES : (n + 1) * LANES, :] = block.T
                index += 1
    for which in range(2):
        for b in range(ATOMS_G):
            for half in range(NAO // slots):
                total = None
                for s in range(slots):
                    rows = pl.ds(first + half * slots + s, own, stride=NAO)
                    piece = full[which, b // slots, rows, :]
                    shift = (s - b % slots) * NAO % LANES
                    if shift:
                        piece = pltpu.roll(piece, shift, 1)
                    total = piece if total is None else jnp.where(lane_slot == s, piece, total)
                tiles[which, half, pl.ds(b, own, stride=ATOMS_G), :] = total
    for half in range(NAO // slots):
        lanes = pl.ds(half * LANES, LANES)
        plus, minus = tiles[0, half], tiles[1, half]
        for k in range(re_ref.shape[0]):
            re_ref[k, :, lanes] = coef[k, 0] * plus + coef[k, 1] * minus
            im_ref[k, :, lanes] = coef[k, 2] * plus + coef[k, 3] * minus


def bloch_tiles(coef, core, blocks, tile_rows):
    shape = jax.ShapeDtypeStruct((coef.shape[0], tile_rows, NAO * NAO), jnp.float32)
    vmem = pl.BlockSpec(memory_space=pltpu.VMEM)
    smem = pl.BlockSpec(memory_space=pltpu.SMEM)
    return pl.pallas_call(
        tile_kernel,
        out_shape=(shape, shape),
        in_specs=[smem, smem, vmem],
        out_specs=(vmem, vmem),
        scratch_shapes=[
            pltpu.VMEM((2, PARTS, ROWS, LANES), jnp.float32),
            pltpu.VMEM((2, NAO * NAO // LANES, tile_rows, LANES), jnp.float32),
        ],
        compiler_params=pltpu.CompilerParams(vmem_limit_bytes=40 << 20),
    )(coef, core, blocks)


def phase_coefficients(phase_index, per_pool):
    mine = lax.dynamic_slice_in_dim(phase_index, lax.axis_index("pool") * per_pool, per_pool, 0)
    angle = mine.astype(jnp.float32) * (2.0 * math.pi / KGRID)
    cos, sin = jnp.cos(angle) * 0.5, jnp.sin(angle) * 0.5
    return jnp.stack(
        [cos[:, 0] + cos[:, 1], cos[:, 0] - cos[:, 1], sin[:, 0] + sin[:, 1], sin[:, 0] - sin[:, 1]], axis=1
    )


def per_device(pot_slab, orbitals, batch_atoms, batch_images, phase_index):
    grid_size = lax.axis_size("grid")
    pool_size = lax.axis_size("pool")
    blk_size = lax.axis_size("blk")
    potential = batch_potential(pot_slab, grid_size)
    blocks = pair_matrices(orbitals, potential, batch_atoms, batch_images)
    summed = summed_blocks(blocks, pool_size)
    coef = phase_coefficients(phase_index, phase_index.shape[0] // pool_size)
    core = jnp.reshape(lax.axis_index("blk"), (1,)).astype(jnp.int32)
    return bloch_tiles(coef, core, summed, ATOMS_G * ATOMS_G // blk_size)


def solution(mesh):
    in_specs = (
        P(("pool", "grid", "blk"), None),
        P(("pool", "grid", "blk"), None, None),
        P(("pool", "grid", "blk"), None),
        P(("pool", "grid", "blk"), None),
        P(),
    )
    out_specs = (P("pool", ("grid", "blk"), None), P("pool", ("grid", "blk"), None))
    return jax.shard_map(
        per_device, mesh=mesh, in_specs=in_specs, out_specs=out_specs, check_vma=False
    )
```

```python
import functools
import math

import jax
import jax.numpy as jnp
from jax import lax
from jax.experimental import pallas as pl
from jax.experimental.pallas import tpu as pltpu
from jax.sharding import PartitionSpec as P

NAO = 16
BATOMS = 16
ATOMS_G = 24
NR = 2
KGRID = 8
CHUNK = 16
LANES = 128
ROWS = ATOMS_G * NAO
PARTS = ROWS // LANES
BLOCKS = PARTS * (PARTS + 1) // 2
PIECES = 6
SKEW = 2
MESH = pl.DeviceIdType.MESH


def swap_kernel(size, slab_ref, orb_ref, out_ref, orb_out, pot_ref, send, land, send_sem, recv_sem, local_sem):
    me = lax.axis_index("grid")
    barrier = pltpu.get_barrier_semaphore()
    for d in range(1, size):
        pl.semaphore_signal(barrier, inc=1, device_id={"grid": lax.rem(me + d, size)}, device_id_type=MESH)
    slab_copy = pltpu.make_async_copy(slab_ref, pot_ref, local_sem.at[0])
    orb_copy = pltpu.make_async_copy(orb_ref, orb_out, local_sem.at[1])
    slab_copy.start()
    orb_copy.start()
    slab_copy.wait()
    rows = pot_ref.shape[0] // size
    for j in range(size):
        send[j] = pot_ref[j * rows : (j + 1) * rows, :]
    pl.semaphore_wait(barrier, size - 1)
    copies = []
    for d in range(1, size):
        to = lax.rem(me + d, size)
        copies.append(
            pltpu.make_async_remote_copy(
                src_ref=send.at[to],
                dst_ref=land.at[d],
                send_sem=send_sem.at[d],
                recv_sem=recv_sem.at[d],
                device_id={"grid": to},
                device_id_type=MESH,
            )
        )
        copies[-1].start()
    land[0] = send[me]
    for copy in copies:
        copy.wait()
    for j in range(size):
        out_ref[j * rows : (j + 1) * rows, :] = land[lax.rem(me - j + size, size)]
    orb_copy.wait()


def batch_potential(pot_slab, orbitals, size):
    rows, points = pot_slab.shape
    vmem = pl.BlockSpec(memory_space=pltpu.VMEM)
    return pl.pallas_call(
        functools.partial(swap_kernel, size),
        out_shape=(
            jax.ShapeDtypeStruct(pot_slab.shape, pot_slab.dtype),
            jax.ShapeDtypeStruct(orbitals.shape, orbitals.dtype),
        ),
        in_specs=[pl.BlockSpec(memory_space=pltpu.HBM)] * 2,
        out_specs=(vmem, vmem),
        scratch_shapes=[pltpu.VMEM(pot_slab.shape, jnp.float32)]
        + [pltpu.VMEM((size, rows // size, points), jnp.float32)] * 2
        + [pltpu.SemaphoreType.DMA((size,))] * 2
        + [pltpu.SemaphoreType.DMA((2,))],
        compiler_params=pltpu.CompilerParams(
            collective_id=0, has_side_effects=True, vmem_limit_bytes=16 << 20
        ),
    )(pot_slab, orbitals)


def pair_kernel(places, orb_ref, pot_ref, out_ref, x, w, sx, sw):
    step = pl.program_id(0)
    points = orb_ref.shape[2]
    for ref in (x, w, sx, sw):
        ref[...] = jnp.zeros_like(ref)
    for c in range(CHUNK):
        batch = step * CHUNK + c
        value = pot_ref[pl.ds(batch, 1), :]
        cols = pl.ds(c * points, points)
        for i in range(BATOMS):
            place = places[batch, i]
            rows = pl.ds(pl.multiple_of((place >> 1) * NAO, NAO), NAO)
            sign = (1 - 2 * (place & 1)).astype(jnp.float32)
            tile = orb_ref[c, i * NAO : (i + 1) * NAO, :]
            wide = tile.astype(jnp.float32)
            weighted = wide * value
            x[rows, cols] = tile
            w[rows, cols] = weighted.astype(jnp.bfloat16)
            sx[rows, cols] = (wide * sign).astype(jnp.bfloat16)
            sw[rows, cols] = (weighted * sign).astype(jnp.bfloat16)

    @pl.when(step == 0)
    def _():
        out_ref[...] = jnp.zeros_like(out_ref)

    for which, (left, right) in enumerate(((w, x), (sw, sx))):
        whole = lax.dot_general(left[...], right[...], (((1,), (1,)), ((), ())), preferred_element_type=jnp.float32)
        index = 0
        for r in range(PARTS):
            for n in range(r, PARTS):
                out_ref[which, index] += whole[r * LANES : (r + 1) * LANES, n * LANES : (n + 1) * LANES]
                index += 1


def pair_matrices(orbitals, potential, batch_atoms, batch_images):
    batches, rows, points = orbitals.shape
    wide = CHUNK * points
    return pl.pallas_call(
        pair_kernel,
        out_shape=jax.ShapeDtypeStruct((2, BLOCKS, LANES, LANES), jnp.float32),
        grid_spec=pltpu.PrefetchScalarGridSpec(
            num_scalar_prefetch=1,
            grid=(batches // CHUNK,),
            in_specs=[
                pl.BlockSpec((CHUNK, rows, points), lambda s, *_: (s, 0, 0)),
                pl.BlockSpec((batches, points), lambda s, *_: (0, 0)),
            ],
            out_specs=pl.BlockSpec((2, BLOCKS, LANES, LANES), lambda s, *_: (0,) * 4),
            scratch_shapes=[pltpu.VMEM((ROWS, wide), jnp.bfloat16)] * 4,
        ),
        compiler_params=pltpu.CompilerParams(vmem_limit_bytes=40 << 20),
    )(batch_atoms * NR + batch_images, orbitals, potential)


def sum_kernel(
    size, mine_ref, out_ref, from_core, own, from_left, from_right, to_right, to_left, other, sends, recvs
):
    pieces = mine_ref.shape[1]
    me, core = lax.axis_index("pool"), lax.axis_index("blk")
    right, left = lax.rem(me + 1, size), lax.rem(me + size - 1, size)
    has_left, has_right = me > 0, me < size - 1
    barrier = pltpu.get_barrier_semaphore()
    for there in ({"blk": 1 - core}, {"pool": left}, {"pool": right}):
        pl.semaphore_signal(barrier, inc=1, device_id=there, device_id_type=MESH)

    def copy(way, src, dst, c, there):
        return pltpu.make_async_remote_copy(
            src_ref=src,
            dst_ref=dst.at[c],
            send_sem=sends.at[way, c],
            recv_sem=recvs.at[way, c],
            device_id=there,
            device_id_type=MESH,
        )

    def core_copy(c):
        return copy(0, mine_ref.at[1 - core, c], from_core, c, {"blk": 1 - core})

    def right_copy(c):
        return copy(1, to_right.at[c], from_left, c, {"pool": right})

    def left_copy(c):
        return copy(2, to_left.at[c], from_right, c, {"pool": left})

    def swap_copy(c):
        return copy(3, out_ref.at[core, c], other, c, {"blk": 1 - core})

    pl.semaphore_wait(barrier, 3)
    for c in range(pieces):
        core_copy(c).start()

    @pl.when(me == 0)
    def _():
        from_left[...] = jnp.zeros_like(from_left)

    @pl.when(me == size - 1)
    def _():
        from_right[...] = jnp.zeros_like(from_right)

    behind = size - 1 - me
    near, far = jnp.minimum(me, behind), jnp.maximum(me, behind)

    def step(t, carry):
        c0, c1, c2, c3 = t - SKEW * near, t - SKEW * me, t - SKEW * behind, t - SKEW * far

        @pl.when((c0 >= 0) & (c0 < pieces))
        def _():
            core_copy(c0).wait_recv()
            own[c0] = mine_ref[core, c0] + from_core[c0]

        @pl.when((c1 >= 0) & (c1 < pieces))
        def _():
            @pl.when(has_left)
            def _():
                right_copy(c1).wait_recv()

            @pl.when(has_right)
            def _():
                to_right[c1] = own[c1] + from_left[c1]
                right_copy(c1).start()

        @pl.when((c2 >= 0) & (c2 < pieces))
        def _():
            @pl.when(has_right)
            def _():
                left_copy(c2).wait_recv()

            @pl.when(has_left)
            def _():
                to_left[c2] = own[c2] + from_right[c2]
                left_copy(c2).start()

        @pl.when((c3 >= 0) & (c3 < pieces))
        def _():
            out_ref[core, c3] = from_left[c3] + own[c3] + from_right[c3]
            swap_copy(c3).start()

        return carry

    lax.fori_loop(0, pieces + SKEW * (size - 1), step, 0)
    for c in range(pieces):
        core_copy(c).wait_send()

        @pl.when(has_right)
        def _():
            right_copy(c).wait_send()

        @pl.when(has_left)
        def _():
            left_copy(c).wait_send()

        swap_copy(c).wait()
        out_ref[1 - core, c] = other[c]


def summed_blocks(blocks, size):
    vmem = pl.BlockSpec(memory_space=pltpu.VMEM)
    pieces = (PIECES, BLOCKS * LANES // PIECES, LANES)
    summed = pl.pallas_call(
        functools.partial(sum_kernel, size),
        out_shape=jax.ShapeDtypeStruct((2, *pieces), blocks.dtype),
        in_specs=[vmem],
        out_specs=vmem,
        scratch_shapes=[pltpu.VMEM(pieces, jnp.float32)] * 7
        + [pltpu.SemaphoreType.DMA((4, PIECES))] * 2,
        compiler_params=pltpu.CompilerParams(
            collective_id=1, has_side_effects=True, vmem_limit_bytes=40 << 20
        ),
    )(blocks.reshape(2, *pieces))
    return summed.reshape(blocks.shape)


def tile_kernel(coef, core, blocks_ref, re_ref, im_ref, full, tiles):
    own = re_ref.shape[1] // ATOMS_G
    slots = LANES // NAO
    first = core[0] * (own * NAO)
    lane_slot = lax.broadcasted_iota(jnp.int32, (own, LANES), 1) // NAO
    for which in range(2):
        index = 0
        for r in range(PARTS):
            for n in range(r, PARTS):
                block = blocks_ref[which, index]
                full[which, n, r * LANES : (r + 1) * LANES, :] = block
                if n > r:
                    full[which, r, n * LANES : (n + 1) * LANES, :] = block.T
                index += 1
    for which in range(2):
        for b in range(ATOMS_G):
            for half in range(NAO // slots):
                total = None
                for s in range(slots):
                    rows = pl.ds(first + half * slots + s, own, stride=NAO)
                    piece = full[which, b // slots, rows, :]
                    shift = (s - b % slots) * NAO % LANES
                    if shift:
                        piece = pltpu.roll(piece, shift, 1)
                    total = piece if total is None else jnp.where(lane_slot == s, piece, total)
                tiles[which, half, pl.ds(b, own, stride=ATOMS_G), :] = total
    for half in range(NAO // slots):
        lanes = pl.ds(half * LANES, LANES)
        plus, minus = tiles[0, half], tiles[1, half]
        for k in range(re_ref.shape[0]):
            re_ref[k, :, lanes] = coef[k, 0] * plus + coef[k, 1] * minus
            im_ref[k, :, lanes] = coef[k, 2] * plus + coef[k, 3] * minus


def bloch_tiles(coef, core, blocks, tile_rows):
    shape = jax.ShapeDtypeStruct((coef.shape[0], tile_rows, NAO * NAO), jnp.float32)
    vmem = pl.BlockSpec(memory_space=pltpu.VMEM)
    smem = pl.BlockSpec(memory_space=pltpu.SMEM)
    return pl.pallas_call(
        tile_kernel,
        out_shape=(shape, shape),
        in_specs=[smem, smem, vmem],
        out_specs=(vmem, vmem),
        scratch_shapes=[
            pltpu.VMEM((2, PARTS, ROWS, LANES), jnp.float32),
            pltpu.VMEM((2, NAO * NAO // LANES, tile_rows, LANES), jnp.float32),
        ],
        compiler_params=pltpu.CompilerParams(vmem_limit_bytes=40 << 20),
    )(coef, core, blocks)


def phase_coefficients(phase_index, per_pool):
    mine = lax.dynamic_slice_in_dim(phase_index, lax.axis_index("pool") * per_pool, per_pool, 0)
    angle = mine.astype(jnp.float32) * (2.0 * math.pi / KGRID)
    cos, sin = jnp.cos(angle) * 0.5, jnp.sin(angle) * 0.5
    return jnp.stack(
        [cos[:, 0] + cos[:, 1], cos[:, 0] - cos[:, 1], sin[:, 0] + sin[:, 1], sin[:, 0] - sin[:, 1]], axis=1
    )


def per_device(pot_slab, orbitals, batch_atoms, batch_images, phase_index):
    grid_size = lax.axis_size("grid")
    pool_size = lax.axis_size("pool")
    blk_size = lax.axis_size("blk")
    potential, near_orbitals = batch_potential(pot_slab, orbitals, grid_size)
    blocks = pair_matrices(near_orbitals, potential, batch_atoms, batch_images)
    summed = summed_blocks(blocks, pool_size)
    coef = phase_coefficients(phase_index, phase_index.shape[0] // pool_size)
    core = jnp.reshape(lax.axis_index("blk"), (1,)).astype(jnp.int32)
    return bloch_tiles(coef, core, summed, ATOMS_G * ATOMS_G // blk_size)


def solution(mesh):
    in_specs = (
        P(("pool", "grid", "blk"), None),
        P(("pool", "grid", "blk"), None, None),
        P(("pool", "grid", "blk"), None),
        P(("pool", "grid", "blk"), None),
        P(),
    )
    out_specs = (P("pool", ("grid", "blk"), None), P("pool", ("grid", "blk"), None))
    return jax.shard_map(
        per_device, mesh=mesh, in_specs=in_specs, out_specs=out_specs, check_vma=False
    )
```
